256 devices in a mesh: row: 32 (over y, x, core), col: 8 (over z).
Axes of the slice: x: 4, y: 4, z: 8, core: 2. Of those that a mesh axis runs over, the one named last changes fastest.
Arguments:
- inputs: bfloat16 [4096, 6144], P('row', 'col'), may hold values from -6 to 6
- cotangent: bfloat16 [4096, 6144], P('row', 'col'), may hold values from -6 to 6
- saved_pre: bfloat16 [4096, 12288], P('col', 'row'), may hold values from -6 to 6
- weight_in: bfloat16 [6144, 12288], P('col', 'row'), may hold values from -0.078125 to 0.078125
- weight_out: bfloat16 [12288, 6144], P('row', 'col'), may hold values from -0.0546875 to 0.0546875
Outputs:
- input_grad: float32 [4096, 6144], P('row', 'col')
- weight_in_grad: float32 [6144, 12288], P('col', 'row')
- weight_out_grad: float32 [12288, 6144], P('row', 'col')
The draws below stay inside these ranges and needn't reach their ends.
All inputs are finite; a program needn't handle non-finite values.
Results may differ from the reference program's by a relative error of at most 0.027.
Values may be sent and summed in bfloat16 or wider, within the bound.
No kernel may reach another device: no remote copies, remote signals or barrier semaphores. Data moves between devices by JAX's collectives and lax.ppermute only.
A program may use at most 128 MiB of HBM per device.

```python
import jax
import jax.numpy as jnp
from jax import lax

D = 6144
FF = 12288
TOKENS = 4096
N_ROW = 32
N_COL = 8


def strengthened(values, rng, source, target, blocks, factor):
    def block_of(position):
        return (jnp.arange(values.shape[position]) // (values.shape[position] // blocks)).reshape((-1,) + (1,) * (values.ndim - 1 - position))

    one_side = jax.random.permutation(rng, blocks)[block_of(target)]
    far = (block_of(target) + blocks // 2) % blocks
    return jnp.where((block_of(source) == one_side) | (block_of(source) == far), factor * values, values)


def level_of(rng, shape, shards, smallest, top_value):
    gain, own = 1.0, jax.random.fold_in(rng, 6)
    for dim, shards_of in shards:
        steps = jnp.exp(jax.random.uniform(jax.random.fold_in(own, dim), (shards_of,), jnp.float32, smallest / len(shards), top_value / len(shards)))
        gain = gain * jnp.repeat(steps, shape[dim] // shards_of).reshape([-1 if axis == dim else 1 for axis in range(len(shape))])
    return gain


def normal_values(rng, dims, width, most, cuts=(), dtype=jnp.bfloat16):
    entries = width * jax.random.normal(rng, dims, jnp.float32)
    if cuts:
        entries = entries * level_of(rng, dims, cuts, -0.22, 0.18)
    return jnp.clip(entries, -most, most).astype(dtype)


def noise_with(key, shape, width, reach, pieces, heavy, kind=jnp.bfloat16):
    drawn = width * jax.random.normal(key, shape, jnp.float32)
    if pieces:
        drawn = drawn * level_of(key, shape, pieces, -0.22, 0.18)
    return jnp.clip(strengthened(drawn, jax.random.fold_in(key, 3), *heavy), -reach, reach).astype(kind)


def setup_inputs(seed: int = 0) -> dict:
    key_list = jax.random.split(jax.random.key(seed), 6)
    inputs = normal_values(key_list[0], (TOKENS, D), 1.0, 6.0, ((0, 32), (1, 8)))
    cotangent = normal_values(key_list[1], (TOKENS, D), 1.0, 6.0, ((0, 32), (1, 8)))
    saved_pre = noise_with(key_list[2], (TOKENS, FF), 1.0, 6.0, ((0, 8), (1, 32)), (1, 0, 32, 2.75))
    weight_in = normal_values(key_list[3], (D, FF), D ** -0.5, 0.078125, ((0, 8), (1, 32)))
    weight_out = normal_values(key_list[4], (FF, D), FF ** -0.5, 0.0546875, ((0, 32), (1, 8)))
    return dict(inputs=inputs, cotangent=cotangent, saved_pre=saved_pre, weight_in=weight_in, weight_out=weight_out)


root_half = 0.7071067811865476
inverse_root = 0.3989422804014327


def gelu_parts(saved):
    widened = saved.astype(jnp.float32)
    lower_mass = 0.5 * (1.0 + lax.erf(widened * root_half))
    density = inverse_root * jnp.exp(-0.5 * widened * widened)
    return widened * lower_mass, lower_mass + widened * density


def rounded(matrix):
    narrow = lax.optimization_barrier(matrix.astype(jnp.bfloat16))
    return narrow.astype(jnp.float32)


def reference(inputs, cotangent, saved_pre, weight_in, weight_out):
    width_block = D // N_COL
    hidden_grad = jnp.zeros((TOKENS, FF), jnp.float32)
    for column in range(N_COL):
        begin = column * width_block
        width_term = lax.dot_general(cotangent[:, begin:begin + width_block], weight_out[:, begin:begin + width_block], (((1,), (1,)), ((), ())), preferred_element_type=jnp.float32)
        hidden_grad = hidden_grad + rounded(width_term)
    active, slope = gelu_parts(saved_pre)
    activated = active.astype(jnp.bfloat16)
    pre_grad = (hidden_grad * slope).astype(jnp.bfloat16)
    weight_out_grad = lax.dot_general(activated, cotangent, (((0,), (0,)), ((), ())), preferred_element_type=jnp.float32)
    weight_in_grad = lax.dot_general(inputs, pre_grad, (((0,), (0,)), ((), ())), preferred_element_type=jnp.float32)
    unit_block = FF // N_ROW
    input_grad = jnp.zeros((TOKENS, D), jnp.float32)
    for blockrow in range(N_ROW):
        begin = blockrow * unit_block
        unit_term = lax.dot_general(pre_grad[:, begin:begin + unit_block], weight_in[:, begin:begin + unit_block], (((1,), (1,)), ((), ())), preferred_element_type=jnp.float32)
        input_grad = input_grad + rounded(unit_term)
    return input_grad, weight_in_grad, weight_out_grad
```

```python
import jax
import jax.numpy as jnp
from jax import lax
from jax.sharding import PartitionSpec as P

root_half = 0.7071067811865476
inverse_root = 0.3989422804014327
F32 = jnp.float32
BF16 = jnp.bfloat16

CORE_SWAP = [(r, r ^ 1) for r in range(32)]


def plane_pairs(k, first):
    pairs = []
    for r in range(32):
        y, x, core = r // 8, (r // 2) % 4, r % 2
        if (core == 0) == first:
            x ^= k
        else:
            y ^= k
        pairs.append((r, y * 8 + x * 2 + core))
    return pairs


def gelu_parts(saved):
    widened = saved.astype(F32)
    lower_mass = 0.5 * (1.0 + lax.erf(widened * root_half))
    density = inverse_root * jnp.exp(-0.5 * widened * widened)
    return (widened * lower_mass, lower_mass + widened * density)


def at(x, i):
    return lax.dynamic_index_in_dim(x, i, 0, keepdims=False)


def swap(x):
    return lax.ppermute(x, "row", CORE_SWAP)


def halves(shard, core):
    s, n, w = shard.shape
    split = shard.reshape(s, 2, n // 2, w)
    mine = lax.dynamic_index_in_dim(split, core, 1, keepdims=False)
    other = lax.dynamic_index_in_dim(split, 1 - core, 1, keepdims=False)
    return mine, other


def body(inputs, cotangent, saved_pre, weight_in, weight_out):
    row = lax.axis_index("row")
    y, x, core = row // 8, (row // 2) % 4, row % 2
    i1 = jnp.where(core == 0, x, y)
    i2 = jnp.where(core == 0, y, x)

    def flat(a2, a1):
        return jnp.where(core == 0, a2 * 4 + a1, a1 * 4 + a2)

    def both_shards(shard):
        mine, other = halves(shard[None], core)
        got = swap(other[0])
        pair = jnp.stack([mine[0], mine[0]])
        return lax.dynamic_update_index_in_dim(pair, got, 1 - core, 0)

    cot_pair = both_shards(cotangent)
    rows = cot_pair.shape[0] * cot_pair.shape[1]
    width = cot_pair.shape[2]
    cot_pair = cot_pair.reshape(rows, width)

    def plane_gather(block):
        first = [block] + [lax.ppermute(block, "row", plane_pairs(k, True)) for k in (1, 2, 3)]
        line = jnp.stack(first)
        second = [line] + [lax.ppermute(line, "row", plane_pairs(k, False)) for k in (1, 2, 3)]
        whole = jnp.zeros((16, rows, width), block.dtype)
        for k2 in range(4):
            for k1 in range(4):
                whole = lax.dynamic_update_index_in_dim(whole, second[k2][k1], flat(i2 ^ k2, i1 ^ k1), 0)
        return whole

    cot_all = plane_gather(cot_pair)

    out_weights = jnp.concatenate([weight_out, swap(weight_out)], 0)
    in_weights = jnp.concatenate([weight_in, swap(weight_in)], 1)
    hidden = out_weights.shape[0]

    saved_mine, saved_other = halves(saved_pre.reshape(4, -1, saved_pre.shape[1]), core)
    saved = jnp.concatenate([saved_mine, swap(saved_other)], 2).reshape(-1, hidden)
    active, slope = gelu_parts(saved)
    active_all = lax.all_gather(active.astype(BF16), "col", axis=0, tiled=True)

    hidden_grad = lax.psum_scatter(
        lax.dot_general(
            cot_all.reshape(-1, width), out_weights, (((1,), (1,)), ((), ())), preferred_element_type=F32
        ).astype(BF16),
        "col",
        scatter_dimension=0,
        tiled=True,
    ).astype(F32)

    same_core = [[r for r in range(32) if r % 2 == k] for k in (0, 1)]
    in_pair = both_shards(inputs).reshape(rows, width)
    in_all = lax.all_gather(in_pair, "row", axis=0, tiled=True, axis_index_groups=same_core)

    grad_all = lax.all_gather((hidden_grad * slope).astype(BF16), "col", axis=0, tiled=True)

    def weight_term(a, b, mine_axis):
        full = lax.dot_general(a, b, (((0,), (0,)), ((), ())), preferred_element_type=F32)
        mine, other = jnp.split(full, 2, mine_axis)
        return mine + swap(other)

    out_grad = weight_term(active_all, cot_all.reshape(-1, width), 0)

    token_grad = lax.dot_general(
        grad_all, in_weights, (((1,), (1,)), ((), ())), preferred_element_type=F32
    ).reshape(16, rows, width)
    token_bf = token_grad.astype(BF16)

    def pieces(k2):
        return jnp.stack([at(token_bf, flat(i2 ^ k2, i1 ^ k1)) for k1 in range(4)])

    line = pieces(0).astype(F32)
    for got in [lax.ppermute(pieces(k), "row", plane_pairs(k, False)) for k in (2, 1, 3)]:
        line = line + got.astype(F32)
    line_bf = line.astype(BF16)
    total = line[0]
    for got in [lax.ppermute(line_bf[k], "row", plane_pairs(k, True)) for k in (2, 1, 3)]:
        total = total + got.astype(F32)
    total = total.reshape(2, rows // 2, width)
    mine = at(total, core)
    got = swap(at(total, 1 - core))
    pair = lax.dynamic_update_index_in_dim(jnp.stack([mine, mine]), got, 1 - core, 0)
    entry_grad = weight_term(in_all, grad_all, 1)
    return (pair.reshape(rows, width), entry_grad, out_grad)


def solution(mesh):
    in_specs = (P("row", "col"), P("row", "col"), P("col", "row"), P("col", "row"), P("row", "col"))
    out_specs = (P("row", "col"), P("col", "row"), P("row", "col"))
    return jax.shard_map(body, mesh=mesh, in_specs=in_specs, out_specs=out_specs, check_vma=False)
```

```python
import jax
import jax.numpy as jnp
from jax import lax
from jax.sharding import PartitionSpec as P

root_half = 0.7071067811865476
inverse_root = 0.3989422804014327
F32 = jnp.float32
BF16 = jnp.bfloat16

CORE_SWAP = [(r, r ^ 1) for r in range(32)]
TRANSPOSE = [(r, r if r % 2 == 0 else (r // 2) % 4 * 8 + r // 8 * 2 + 1) for r in range(32)]
RING = ([(c, c ^ 1) for c in range(8)], [(c, (c - 1) % 8 if c % 2 == 0 else (c + 1) % 8) for c in range(8)])


def plane_pairs(k, first):
    pairs = []
    for r in range(32):
        y, x, core = r // 8, (r // 2) % 4, r % 2
        if (core == 0) == first:
            x ^= k
        else:
            y ^= k
        pairs.append((r, y * 8 + x * 2 + core))
    return pairs


def gelu_parts(saved):
    widened = saved.astype(F32)
    lower_mass = 0.5 * (1.0 + lax.erf(widened * root_half))
    density = inverse_root * jnp.exp(-0.5 * widened * widened)
    return (widened * lower_mass, lower_mass + widened * density)


def at(x, i):
    return lax.dynamic_index_in_dim(x, i, 0, keepdims=False)


def put(x, piece, i):
    return lax.dynamic_update_index_in_dim(x, piece, i, 0)


def swap(x):
    return lax.ppermute(x, "row", CORE_SWAP)


def dot_rows(a, b):
    return lax.dot_general(a, b, (((1,), (1,)), ((), ())), preferred_element_type=F32)


def halves(shard, core):
    s, n, w = shard.shape
    split = shard.reshape(s, 2, n // 2, w)
    mine = lax.dynamic_index_in_dim(split, core, 1, keepdims=False)
    other = lax.dynamic_index_in_dim(split, 1 - core, 1, keepdims=False)
    return mine, other


def body(inputs, cotangent, saved_pre, weight_in, weight_out):
    row, col = lax.axis_index("row"), lax.axis_index("col")
    y, x, core = row // 8, (row // 2) % 4, row % 2
    i1 = jnp.where(core == 0, x, y)
    i2 = jnp.where(core == 0, y, x)
    sign = 1 - 2 * (col % 2)

    def both_shards(shard):
        mine, other = halves(shard[None], core)
        got = swap(other[0])
        pair = jnp.stack([mine[0], mine[0]])
        return put(pair, got, 1 - core).reshape(-1, shard.shape[1])

    cot_pair = both_shards(cotangent)
    rows, width = cot_pair.shape

    out_weights = jnp.concatenate([weight_out, swap(weight_out)], 0)
    in_weights = jnp.concatenate([weight_in, swap(weight_in)], 1)
    hidden = out_weights.shape[0]

    saved_mine, saved_other = halves(saved_pre.reshape(4, -1, saved_pre.shape[1]), core)
    saved = jnp.concatenate([saved_mine, swap(saved_other)], 2).reshape(2, rows, hidden)
    active, slope = gelu_parts(saved)
    active, slope = lax.optimization_barrier((active.astype(BF16), slope))
    active_all = lax.all_gather(active.reshape(-1, hidden), "col", axis=0, tiled=True)

    line = jnp.zeros((4, rows, width), BF16)
    line = put(line, cot_pair, i1)
    for k in (2, 1, 3):
        line = put(line, lax.ppermute(cot_pair, "row", plane_pairs(k, True)), i1 ^ k)
    second = {0: line}
    for k in (2, 1, 3):
        second[k] = lax.ppermute(line, "row", plane_pairs(k, False))
    partial = jnp.zeros((4, 4 * rows, hidden), BF16)
    for k in (0, 1, 3, 2):
        partial = put(partial, dot_rows(second[k].reshape(-1, width), out_weights).astype(BF16), i2 ^ k)
    partial = partial.reshape(16, rows, hidden)

    def place(step, chunk):
        block = (col + step * sign) % 8
        by, bx = block // 2, 2 * (block % 2) + chunk
        return jnp.where(core == 0, by * 4 + bx, bx * 4 + by)

    def hop(a, side):
        return lax.ppermute(a, "col", RING[side])

    chunks = (0, 1)
    half = rows // 2
    got = {}
    for j in chunks:
        far = at(partial, place(4, j))
        got[j] = [hop(far[:half], 0), hop(far[half:], 1)]
    for step in (3, 2, 1):
        for j in chunks:
            from_0, from_1 = got[j][0].astype(F32), got[j][1].astype(F32)
            go_0 = at(partial, place(step, j)).astype(F32)
            go_1 = at(partial, place(-step, j)).astype(F32)
            if step == 3:
                go_0 = jnp.concatenate([go_0[:half], go_0[half:] + from_1], 0)
                go_1 = jnp.concatenate([go_1[:half] + from_0, go_1[half:]], 0)
            else:
                go_0, go_1 = go_0 + from_1, go_1 + from_0
            got[j] = [hop(go_0.astype(BF16), 0), hop(go_1.astype(BF16), 1)]

    grad_all = jnp.zeros((16, rows, hidden), BF16)
    sent = {}
    for j in chunks:
        summed = at(partial, place(0, j)).astype(F32) + got[j][0].astype(F32) + got[j][1].astype(F32)
        grad = (summed * slope[j]).astype(BF16)
        grad_all = put(grad_all, grad, place(0, j))
        sent[j] = [grad, grad]
    for step in (1, 2, 3):
        for j in chunks:
            from_0, from_1 = hop(sent[j][0], 0), hop(sent[j][1], 1)
            grad_all = put(grad_all, from_0, place(step, j))
            grad_all = put(grad_all, from_1, place(-step, j))
            sent[j] = [from_1, from_0]
    for j in chunks:
        both = jnp.concatenate([hop(sent[j][0][:half], 0), hop(sent[j][1][half:], 1)], 0)
        grad_all = put(grad_all, both, place(4, j))

    grad_lines = grad_all.reshape(4, 4 * rows, hidden)

    def token_line(k):
        return dot_rows(at(grad_lines, i2 ^ k), in_weights)

    arrived = [lax.ppermute(token_line(k).astype(BF16), "row", plane_pairs(k, False)) for k in (2, 1, 3)]
    mid = token_line(0)
    for got_line in arrived:
        mid = mid + got_line.astype(F32)
    mid = mid.reshape(4, rows, width)
    total = at(mid, i1)
    for k in (2, 1, 3):
        total = total + lax.ppermute(at(mid, i1 ^ k).astype(BF16), "row", plane_pairs(k, True)).astype(F32)
    total = total.reshape(2, rows // 2, width)
    mine = at(total, core)
    token_grad = put(jnp.stack([mine, mine]), swap(at(total, 1 - core)), 1 - core).reshape(rows, width)

    def weight_term(a, b, axis):
        full = lax.dot_general(a, b, (((0,), (0,)), ((), ())), preferred_element_type=F32)
        mine, other = jnp.split(full, 2, axis)
        return mine + swap(other)

    cot_all = jnp.zeros((16, rows, width), BF16)
    for k2 in range(4):
        for k1 in range(4):
            a2, a1 = i2 ^ k2, k1
            cot_all = put(cot_all, second[k2][k1], jnp.where(core == 0, a2 * 4 + a1, a1 * 4 + a2))
    out_grad = weight_term(active_all, cot_all.reshape(-1, width), 0)

    in_pair = both_shards(inputs)
    in_pair, _ = lax.optimization_barrier((in_pair, active_all))
    in_pair = lax.ppermute(in_pair, "row", TRANSPOSE)
    groups = [[r for r in range(32) if r % 2 == k] for k in (0, 1)]
    in_all = lax.all_gather(in_pair, "row", axis=0, tiled=True, axis_index_groups=groups)
    entry_grad = weight_term(in_all, grad_all.reshape(-1, hidden), 1)
    return (token_grad, entry_grad, out_grad)


def solution(mesh):
    in_specs = (P("row", "col"), P("row", "col"), P("col", "row"), P("col", "row"), P("row", "col"))
    out_specs = (P("row", "col"), P("col", "row"), P("row", "col"))
    return jax.shard_map(body, mesh=mesh, in_specs=in_specs, out_specs=out_specs, check_vma=False)
```

```python
import jax
import jax.numpy as jnp
from jax import lax
from jax.experimental import pallas as pl
from jax.experimental.pallas import tpu as pltpu
from jax.sharding import PartitionSpec as P

root_half = 0.7071067811865476
inverse_root = 0.3989422804014327
F32 = jnp.float32
BF16 = jnp.bfloat16

CORE_SWAP = [(r, r ^ 1) for r in range(32)]
RING = ([(c, c ^ 1) for c in range(8)], [(c, (c - 1) % 8 if c % 2 == 0 else (c + 1) % 8) for c in range(8)])


def plane_pairs(k, first):
    pairs = []
    for r in range(32):
        y, x, core = r // 8, (r // 2) % 4, r % 2
        if (core == 0) == first:
            x ^= k
        else:
            y ^= k
        pairs.append((r, y * 8 + x * 2 + core))
    return pairs


def gelu_parts(saved):
    widened = saved.astype(F32)
    lower_mass = 0.5 * (1.0 + lax.erf(widened * root_half))
    density = inverse_root * jnp.exp(-0.5 * widened * widened)
    return (widened * lower_mass, lower_mass + widened * density)


def at(x, i):
    return lax.dynamic_index_in_dim(x, i, 0, keepdims=False)


def put(x, piece, i):
    return lax.dynamic_update_index_in_dim(x, piece, i, 0)


def after(x, *others):
    return lax.optimization_barrier((x,) + others)[0]


def swap(x):
    return lax.ppermute(x, "row", CORE_SWAP)


def hop(a, side):
    return lax.ppermute(a, "col", RING[side])


def dot_rows(a, b):
    return lax.dot_general(a, b, (((1,), (1,)), ((), ())), preferred_element_type=F32)


def dot_tokens(a, b):
    return lax.dot_general(a, b, (((0,), (0,)), ((), ())), preferred_element_type=F32)


def scatter(pieces, places, starts, groups, into=None):
    n = len(pieces)
    rows, width = groups[1], groups[2]

    def kernel(*refs):
        table, sources, target, sems = refs[0], refs[1 : 1 + n], refs[-2], refs[-1]
        copies = []
        for i in range(n):
            size = pieces[i].shape[0]
            dst = target.at[table[i], pl.ds(starts[i], size)]
            copies.append(pltpu.make_async_copy(sources[i], dst, sems.at[i]))
        for copy in copies:
            copy.start()
        for copy in copies:
            copy.wait()

    operands = [jnp.stack(places).astype(jnp.int32)] + list(pieces)
    specs = [pl.BlockSpec(memory_space=pltpu.SMEM)] + [pl.BlockSpec(memory_space=pl.ANY)] * n
    aliases = {}
    if into is not None:
        operands.append(into)
        specs.append(pl.BlockSpec(memory_space=pl.ANY))
        aliases = {n + 1: 0}
    return pl.pallas_call(
        kernel,
        out_shape=jax.ShapeDtypeStruct(groups, BF16),
        in_specs=specs,
        out_specs=pl.BlockSpec(memory_space=pl.ANY),
        scratch_shapes=[pltpu.SemaphoreType.DMA((n,))],
        input_output_aliases=aliases,
        cost_estimate=pl.CostEstimate(flops=0, bytes_accessed=4 * sum(p.size for p in pieces), transcendentals=0),
    )(*operands)


def body(inputs, cotangent, saved_pre, weight_in, weight_out):
    row, col = lax.axis_index("row"), lax.axis_index("col")
    y, x, core = row // 8, (row // 2) % 4, row % 2
    i1 = jnp.where(core == 0, x, y)
    i2 = jnp.where(core == 0, y, x)
    sign = 1 - 2 * (col % 2)
    width, units = weight_in.shape
    rows = inputs.shape[0]
    half = rows // 2
    hidden = 2 * units

    def token_half(shard):
        return lax.dynamic_slice_in_dim(shard, core * half, half, 0)

    def pair_of(shard):
        return jnp.concatenate([token_half(shard), token_half(swap(shard))], 0)

    def gather_first(pair):
        line = {k: lax.ppermute(pair, "row", plane_pairs(k, True)) for k in (2, 1, 3)}
        line[0] = pair
        whole = jnp.zeros((4, rows, width), BF16)
        for k in (0, 2, 1, 3):
            whole = put(whole, line[k], i1 ^ k)
        return whole.reshape(4 * rows, width)

    def gather_second(line):
        lines = {k: lax.ppermute(line, "row", plane_pairs(k, False)) for k in (2, 1, 3)}
        lines[0] = line
        return lines

    cot_pair = pair_of(cotangent)
    cot_line = gather_first(cot_pair)
    cot_lines = gather_second(cot_line)

    weight_out_t = after(weight_out, cot_pair)
    out_weights = jnp.concatenate([weight_out_t, swap(weight_out_t)], 0)

    saved_t = after(saved_pre, cot_pair)

    def saved_half(block):
        split = block.reshape(2, 2, 2, half, units)
        split = lax.dynamic_index_in_dim(split, core, 2, keepdims=False)
        own = lax.dynamic_index_in_dim(split, core, 1, keepdims=False)
        other = lax.dynamic_index_in_dim(split, 1 - core, 1, keepdims=False)
        return jnp.concatenate([own, other], 1)

    saved = jnp.concatenate([saved_half(saved_t), saved_half(swap(saved_t))], 2)
    active, slope = gelu_parts(saved)
    active, slope = lax.optimization_barrier((active.astype(BF16), slope))

    partial = jnp.zeros((4, 4 * rows, hidden), BF16)
    for k in (0, 1, 3, 2):
        partial = put(partial, dot_rows(cot_lines[k], out_weights).astype(BF16), k)
    partial = partial.reshape(16, rows, hidden)

    def place(step, chunk):
        block = (col + step * sign) % 8
        by, bx = block // 2, 2 * (block % 2) + chunk
        far = jnp.where(core == 0, by, bx)
        near = jnp.where(core == 0, bx, by)
        return (far ^ i2) * 4 + near

    active_pieces, active_places = [active[0], active[1]], [place(0, 0), place(0, 1)]
    go = [active, active]
    for step in (1, 2, 3):
        from_0, from_1 = hop(go[0], 0), hop(go[1], 1)
        for chunk in (0, 1):
            active_pieces += [from_0[chunk], from_1[chunk]]
            active_places += [place(step, chunk), place(-step, chunk)]
        go = [from_1, from_0]
    active_pieces += [hop(go[0][0], 0), hop(go[1][1], 1)]
    active_places += [place(4, 0), place(4, 1)]

    chunks = (0, 1)
    got = {}
    for j in chunks:
        far = at(partial, place(4, j))
        got[j] = [hop(far[:half], 0), hop(far[half:], 1)]
    for step in (3, 2, 1):
        for j in chunks:
            from_0, from_1 = got[j][0].astype(F32), got[j][1].astype(F32)
            go_0 = at(partial, place(step, j)).astype(F32)
            go_1 = at(partial, place(-step, j)).astype(F32)
            if step == 3:
                go_0 = jnp.concatenate([go_0[:half], go_0[half:] + from_1], 0)
                go_1 = jnp.concatenate([go_1[:half] + from_0, go_1[half:]], 0)
            else:
                go_0, go_1 = go_0 + from_1, go_1 + from_0
            got[j] = [hop(go_0.astype(BF16), 0), hop(go_1.astype(BF16), 1)]

    grad_pieces, grad_places = [], []
    sent = {}
    for j in chunks:
        summed = at(partial, place(0, j)).astype(F32) + got[j][0].astype(F32) + got[j][1].astype(F32)
        grad = (summed * slope[j]).astype(BF16)
        grad_pieces.append(grad)
        grad_places.append(place(0, j))
        sent[j] = [grad, grad]
    for step in (1, 2, 3):
        for j in chunks:
            from_0, from_1 = hop(sent[j][0], 0), hop(sent[j][1], 1)
            grad_pieces += [from_0, from_1]
            grad_places += [place(step, j), place(-step, j)]
            sent[j] = [from_1, from_0]
    groups = (16, rows, hidden)
    grad_all = scatter(grad_pieces, grad_places, [0] * 14, groups)
    last = [hop(sent[j][s][s * half : (s + 1) * half], s) for j in chunks for s in (0, 1)]
    grad_all = scatter(last, [place(4, 0)] * 2 + [place(4, 1)] * 2, [0, half, 0, half], groups, grad_all)
    grad_lines = grad_all.reshape(4, 4 * rows, hidden)

    in_weights = jnp.concatenate([weight_in, swap(after(weight_in, cot_lines[2]))], 1)
    arrived = []
    for k in (2, 1, 3):
        line = dot_rows(grad_lines[k], in_weights).astype(BF16)
        arrived.append(lax.ppermute(line, "row", plane_pairs(k, False)))
    last_line = line
    mid = dot_rows(grad_lines[0], in_weights)
    for got_line in arrived:
        mid = mid + got_line.astype(F32)
    mid = mid.reshape(4, rows, width)
    total = at(mid, i1)
    for k in (2, 1, 3):
        total = total + lax.ppermute(at(mid, i1 ^ k).astype(BF16), "row", plane_pairs(k, True)).astype(F32)
    own, other = total[:half], swap(total[half:])
    token_grad = jnp.where(core == 0, jnp.concatenate([own, other], 0), jnp.concatenate([other, own], 0))

    active_pieces = [after(p, last_line) for p in active_pieces]
    active_all = scatter(active_pieces, active_places, [0] * 16, groups).reshape(4, 4 * rows, hidden)
    out_other = sum(dot_tokens(active_all[k][:, units:], cot_lines[k]) for k in range(4))
    out_own = sum(dot_tokens(active_all[k][:, :units], cot_lines[k]) for k in range(4))
    out_grad = out_own + swap(out_other)

    in_lines = gather_second(gather_first(pair_of(after(inputs, cot_lines[2]))))
    in_other = sum(dot_tokens(in_lines[k], grad_lines[k][:, units:]) for k in range(4))
    in_own = sum(dot_tokens(in_lines[k], grad_lines[k][:, :units]) for k in range(4))
    entry_grad = in_own + swap(in_other)
    return (token_grad, entry_grad, out_grad)


def solution(mesh):
    in_specs = (P("row", "col"), P("row", "col"), P("col", "row"), P("col", "row"), P("row", "col"))
    out_specs = (P("row", "col"), P("col", "row"), P("row", "col"))
    return jax.shard_map(body, mesh=mesh, in_specs=in_specs, out_specs=out_specs, check_vma=False)
```

```python
import jax
import jax.numpy as jnp
from jax import lax
from jax.sharding import PartitionSpec as P

root_half = 0.7071067811865476
inverse_root = 0.3989422804014327
F32 = jnp.float32
BF16 = jnp.bfloat16

CORE_SWAP = [(r, r ^ 1) for r in range(32)]
RING = ([(c, c ^ 1) for c in range(8)], [(c, (c - 1) % 8 if c % 2 == 0 else (c + 1) % 8) for c in range(8)])


def plane_pairs(k, first):
    pairs = []
    for r in range(32):
        y, x, core = r // 8, (r // 2) % 4, r % 2
        if (core == 0) == first:
            x ^= k
        else:
            y ^= k
        pairs.append((r, y * 8 + x * 2 + core))
    return pairs


def gelu_parts(saved):
    widened = saved.astype(F32)
    lower_mass = 0.5 * (1.0 + lax.erf(widened * root_half))
    density = inverse_root * jnp.exp(-0.5 * widened * widened)
    return (widened * lower_mass, lower_mass + widened * density)


def at(x, i):
    return lax.dynamic_index_in_dim(x, i, 0, keepdims=False)


def put(x, piece, i):
    return lax.dynamic_update_index_in_dim(x, piece, i, 0)


def after(x, *others):
    return lax.optimization_barrier((x,) + others)[0]


def swap(x):
    return lax.ppermute(x, "row", CORE_SWAP)


def hop(a, side):
    return lax.ppermute(a, "col", RING[side])


def dot_rows(a, b):
    return lax.dot_general(a, b, (((1,), (1,)), ((), ())), preferred_element_type=F32)


def dot_tokens(a, b):
    return lax.dot_general(a, b, (((0,), (0,)), ((), ())), preferred_element_type=F32)


def body(inputs, cotangent, saved_pre, weight_in, weight_out):
    row, col = lax.axis_index("row"), lax.axis_index("col")
    y, x, core = row // 8, (row // 2) % 4, row % 2
    i1 = jnp.where(core == 0, x, y)
    i2 = jnp.where(core == 0, y, x)
    sign = 1 - 2 * (col % 2)
    width, units = weight_in.shape
    rows = inputs.shape[0]
    half = rows // 2
    hidden = 2 * units

    def token_half(shard):
        return lax.dynamic_slice_in_dim(shard, core * half, half, 0)

    def pair_of(shard):
        return jnp.concatenate([token_half(shard), token_half(swap(shard))], 0)

    def gather_first(pair):
        line = {k: lax.ppermute(pair, "row", plane_pairs(k, True)) for k in (2, 1, 3)}
        line[0] = pair
        whole = jnp.zeros((4, rows, width), BF16)
        for k in (0, 2, 1, 3):
            whole = put(whole, line[k], i1 ^ k)
        return whole.reshape(4 * rows, width)

    def gather_second(line):
        lines = {k: lax.ppermute(line, "row", plane_pairs(k, False)) for k in (2, 1, 3)}
        lines[0] = line
        return lines

    def in_order(lines):
        whole = jnp.zeros((4, 4 * rows, width), BF16)
        for k in (0, 1, 3, 2):
            whole = put(whole, lines[k], i2 ^ k)
        return whole.reshape(16 * rows, width)

    cot_pair = pair_of(cotangent)
    cot_line = gather_first(cot_pair)
    weight_out_t, weight_in_t, inputs_t = lax.optimization_barrier((weight_out, weight_in, inputs, cot_pair))[:3]
    out_weights = jnp.concatenate([weight_out_t, swap(weight_out_t)], 0)

    def saved_half(block):
        split = block.reshape(2, 2, 2, half, units)
        split = lax.dynamic_index_in_dim(split, core, 2, keepdims=False)
        own = lax.dynamic_index_in_dim(split, core, 1, keepdims=False)
        other = lax.dynamic_index_in_dim(split, 1 - core, 1, keepdims=False)
        return jnp.concatenate([own, other], 1)

    saved_t = after(saved_pre, cot_pair)
    saved = jnp.concatenate([saved_half(saved_t), saved_half(swap(saved_t))], 2)
    active, slope = gelu_parts(saved)
    active, slope = lax.optimization_barrier((active.astype(BF16).reshape(2 * rows, hidden), slope))

    cot_lines = gather_second(cot_line)
    partial = jnp.zeros((4, 4 * rows, hidden), BF16)
    partial = put(partial, dot_rows(cot_lines[0], out_weights).astype(BF16), i2)
    active, partial = lax.optimization_barrier((active, partial))
    from_0, from_1 = hop(active, 0), hop(active, 1)
    for k in (1, 3, 2):
        partial = put(partial, dot_rows(cot_lines[k], out_weights).astype(BF16), i2 ^ k)
    partial, from_0, from_1 = lax.optimization_barrier((partial, from_0, from_1))
    partial = partial.reshape(16, rows, hidden)

    def block_at(step):
        return (col + step * sign) % 8

    def place(step, chunk):
        by, bx = block_at(step) // 2, 2 * (block_at(step) % 2) + chunk
        return jnp.where(core == 0, by * 4 + bx, bx * 4 + by)

    def part(step):
        return [at(partial, place(step, chunk)).astype(F32) for chunk in (0, 1)]

    sum_0, sum_1 = hop(at(partial, place(4, 0)), 0), hop(at(partial, place(4, 1)), 1)
    for step in (3, 2, 1):
        go_0, go_1 = part(step), part(-step)
        if step == 3:
            go_0[1], go_1[0] = go_0[1] + sum_1.astype(F32), go_1[0] + sum_0.astype(F32)
        else:
            go_0 = [g + sum_1[j * rows : (j + 1) * rows].astype(F32) for j, g in enumerate(go_0)]
            go_1 = [g + sum_0[j * rows : (j + 1) * rows].astype(F32) for j, g in enumerate(go_1)]
        sum_0 = hop(jnp.concatenate(go_0, 0).astype(BF16), 0)
        sum_1 = hop(jnp.concatenate(go_1, 0).astype(BF16), 1)
    summed = jnp.concatenate(part(0), 0) + sum_0.astype(F32) + sum_1.astype(F32)
    grad = (summed * slope.reshape(2 * rows, hidden)).astype(BF16)

    active_all = put(jnp.zeros((8, 2 * rows, hidden), BF16), active, block_at(0))
    for step in (1, 2, 3):
        active_all = put(active_all, from_0, block_at(step))
        active_all = put(active_all, from_1, block_at(-step))
        if step < 3:
            from_0, from_1 = hop(from_1, 0), hop(from_0, 1)
    ends = jnp.concatenate([hop(from_1[:rows], 0), hop(from_0[rows:], 1)], 0)
    active_all = put(active_all, ends, block_at(4))
    in_pair = pair_of(after(inputs_t, cot_lines[3]))
    in_all = in_order(gather_second(gather_first(in_pair)))
    cot_all = in_order(cot_lines)
    in_weights = jnp.concatenate([weight_in_t, swap(weight_in_t)], 1)

    grad, active_all, in_all, cot_all, in_weights = lax.optimization_barrier(
        (grad, active_all, in_all, cot_all, in_weights)
    )

    chunks = (0, 1)
    sent = {}
    moved = jnp.zeros((16, rows, width), BF16)
    grad_all = jnp.zeros((16, rows, hidden), BF16)

    def take(moved, grad_all, grad, step, chunk):
        spot = place(step, chunk)
        return put(moved, dot_rows(grad, in_weights).astype(BF16), spot), put(grad_all, grad, spot)

    for j in chunks:
        piece = grad[j * rows : (j + 1) * rows]
        moved, grad_all = take(moved, grad_all, piece, 0, j)
        sent[j] = [piece, piece]
    for step in (1, 2, 3):
        for j in chunks:
            from_0, from_1 = hop(sent[j][0], 0), hop(sent[j][1], 1)
            moved, grad_all = take(moved, grad_all, from_0, step, j)
            moved, grad_all = take(moved, grad_all, from_1, -step, j)
            sent[j] = [from_1, from_0]
    for j in chunks:
        ends = [hop(sent[j][s][s * half : (s + 1) * half], s) for s in (0, 1)]
        moved, grad_all = take(moved, grad_all, jnp.concatenate(ends, 0), 4, j)

    lines = moved.reshape(4, 4 * rows, width)
    mid = at(lines, i2).astype(F32)
    for k in (2, 1, 3):
        mid = mid + lax.ppermute(at(lines, i2 ^ k), "row", plane_pairs(k, False)).astype(F32)
    active_all, in_all = lax.optimization_barrier((active_all, in_all, lines))[:2]
    active_all = lax.cond(
        core == 0, lambda a: a, lambda a: jnp.swapaxes(a, 0, 1), active_all.reshape(4, 4, rows, hidden)
    ).reshape(16 * rows, hidden)
    grad_all = grad_all.reshape(16 * rows, hidden)
    parts = (
        dot_tokens(in_all, grad_all[:, units:]),
        dot_tokens(active_all[:, units:], cot_all),
        dot_tokens(in_all, grad_all[:, :units]),
        dot_tokens(active_all[:, :units], cot_all),
    )
    mid, parts = lax.optimization_barrier((mid.reshape(4, rows, width), parts))
    entry_grad = parts[2] + swap(parts[0])
    out_grad = parts[3] + swap(parts[1])
    total = at(mid, i1)
    for k in (2, 1, 3):
        total = total + lax.ppermute(at(mid, i1 ^ k).astype(BF16), "row", plane_pairs(k, True)).astype(F32)
    own, other = total[:half], swap(total[half:])
    token_grad = jnp.where(core == 0, jnp.concatenate([own, other], 0), jnp.concatenate([other, own], 0))
    return (token_grad, entry_grad, out_grad)


def solution(mesh):
    in_specs = (P("row", "col"), P("row", "col"), P("col", "row"), P("col", "row"), P("row", "col"))
    out_specs = (P("row", "col"), P("col", "row"), P("row", "col"))
    return jax.shard_map(body, mesh=mesh, in_specs=in_specs, out_specs=out_specs, check_vma=False)
```

```python
import jax
import jax.numpy as jnp
from jax import lax
from jax.sharding import PartitionSpec as P

root_half = 0.7071067811865476
inverse_root = 0.3989422804014327
F32 = jnp.float32
BF16 = jnp.bfloat16

CORE_SWAP = [(r, r ^ 1) for r in range(32)]
RING = ([(c, c ^ 1) for c in range(8)], [(c, (c - 1) % 8 if c % 2 == 0 else (c + 1) % 8) for c in range(8)])


def plane_pairs(k, first):
    pairs = []
    for r in range(32):
        y, x, core = r // 8, (r // 2) % 4, r % 2
        if (core == 0) == first:
            x ^= k
        else:
            y ^= k
        pairs.append((r, y * 8 + x * 2 + core))
    return pairs


def gelu_parts(saved):
    widened = saved.astype(F32)
    lower_mass = 0.5 * (1.0 + lax.erf(widened * root_half))
    density = inverse_root * jnp.exp(-0.5 * widened * widened)
    return (widened * lower_mass, lower_mass + widened * density)


def at(x, i):
    return lax.dynamic_index_in_dim(x, i, 0, keepdims=False)


def put(x, piece, i):
    return lax.dynamic_update_index_in_dim(x, piece, i, 0)


def after(x, *others):
    return lax.optimization_barrier((x,) + others)[0]


def swap(x):
    return lax.ppermute(x, "row", CORE_SWAP)


def hop(a, side):
    return lax.ppermute(a, "col", RING[side])


def dot_rows(a, b):
    return lax.dot_general(a, b, (((1,), (1,)), ((), ())), preferred_element_type=F32)


def dot_tokens(a, b):
    return lax.dot_general(a, b, (((0,), (0,)), ((), ())), preferred_element_type=F32)


def body(inputs, cotangent, saved_pre, weight_in, weight_out):
    row, col = lax.axis_index("row"), lax.axis_index("col")
    y, x, core = row // 8, (row // 2) % 4, row % 2
    i1 = jnp.where(core == 0, x, y)
    i2 = jnp.where(core == 0, y, x)
    sign = 1 - 2 * (col % 2)
    width, units = weight_in.shape
    rows = inputs.shape[0]
    half = rows // 2
    hidden = 2 * units

    def token_half(shard):
        return lax.dynamic_slice_in_dim(shard, core * half, half, 0)

    def pair_of(shard):
        return jnp.concatenate([token_half(shard), token_half(swap(shard))], 0)

    def gather_first(pair):
        line = {k: lax.ppermute(pair, "row", plane_pairs(k, True)) for k in (2, 1, 3)}
        line[0] = pair
        whole = jnp.zeros((4, rows, width), BF16)
        for k in (0, 2, 1, 3):
            whole = put(whole, line[k], i1 ^ k)
        return whole.reshape(4 * rows, width)

    def gather_second(line):
        lines = {k: lax.ppermute(line, "row", plane_pairs(k, False)) for k in (2, 1, 3)}
        lines[0] = line
        return lines

    def in_order(lines):
        whole = jnp.zeros((4, 4 * rows, width), BF16)
        for k in (0, 1, 3, 2):
            whole = put(whole, lines[k], i2 ^ k)
        return whole.reshape(16 * rows, width)

    cot_pair = pair_of(cotangent)
    cot_line = gather_first(cot_pair)
    weight_out_t, weight_in_t, inputs_t = lax.optimization_barrier((weight_out, weight_in, inputs, cot_pair))[:3]
    out_weights = jnp.concatenate([weight_out_t, swap(weight_out_t)], 0)

    def saved_half(block):
        split = block.reshape(2, 2, 2, half, units)
        split = lax.dynamic_index_in_dim(split, core, 2, keepdims=False)
        own = lax.dynamic_index_in_dim(split, core, 1, keepdims=False)
        other = lax.dynamic_index_in_dim(split, 1 - core, 1, keepdims=False)
        return jnp.concatenate([own, other], 1)

    saved_t = after(saved_pre, cot_pair)
    saved = jnp.concatenate([saved_half(saved_t), saved_half(swap(saved_t))], 2)
    active, slope = gelu_parts(saved)
    active, slope = lax.optimization_barrier((active.astype(BF16).reshape(2 * rows, hidden), slope))

    cot_lines = gather_second(cot_line)
    partial = jnp.zeros((4, 4 * rows, hidden), BF16)
    partial = put(partial, dot_rows(cot_lines[0], out_weights).astype(BF16), i2)
    active, partial = lax.optimization_barrier((active, partial))
    ring = [(active, active)]

    def turn():
        from_0, from_1 = ring[-1]
        ring.append((hop(from_1, 0), hop(from_0, 1)))

    turn()
    for k in (1, 3, 2):
        partial = put(partial, dot_rows(cot_lines[k], out_weights).astype(BF16), i2 ^ k)
    partial, ring[1] = lax.optimization_barrier((partial, ring[1]))
    partial = partial.reshape(16, rows, hidden)

    def block_at(step):
        return (col + step * sign) % 8

    def place(step, chunk):
        by, bx = block_at(step) // 2, 2 * (block_at(step) % 2) + chunk
        return jnp.where(core == 0, by * 4 + bx, bx * 4 + by)

    def part(step):
        return [at(partial, place(step, chunk)).astype(F32) for chunk in (0, 1)]

    def add(step, sum_0, sum_1):
        go_0, go_1 = part(step), part(-step)
        if step == 3:
            go_0[1], go_1[0] = go_0[1] + sum_1.astype(F32), go_1[0] + sum_0.astype(F32)
        else:
            go_0 = [g + sum_1[j * rows : (j + 1) * rows].astype(F32) for j, g in enumerate(go_0)]
            go_1 = [g + sum_0[j * rows : (j + 1) * rows].astype(F32) for j, g in enumerate(go_1)]
        return hop(jnp.concatenate(go_0, 0).astype(BF16), 0), hop(jnp.concatenate(go_1, 0).astype(BF16), 1)

    in_pair = pair_of(after(inputs_t, cot_lines[3]))
    sums = (hop(at(partial, place(4, 0)), 0), hop(at(partial, place(4, 1)), 1))
    turn()
    sums, ring[2], in_pair = lax.optimization_barrier((sums, ring[2], in_pair))

    sums = add(3, *sums)
    in_line = gather_first(in_pair)
    sums, in_line = lax.optimization_barrier((sums, in_line))

    in_lines = gather_second(in_line)
    sums = lax.optimization_barrier(add(2, *sums))

    sums = add(1, *sums)
    sums, in_lines = lax.optimization_barrier((sums, in_lines))
    summed = jnp.concatenate(part(0), 0) + sums[0].astype(F32) + sums[1].astype(F32)
    grad = (summed * slope.reshape(2 * rows, hidden)).astype(BF16)

    in_all = in_order(in_lines)
    cot_all = in_order(cot_lines)
    in_weights = jnp.concatenate([weight_in_t, swap(weight_in_t)], 1)

    grad, in_all, cot_all, in_weights = lax.optimization_barrier((grad, in_all, cot_all, in_weights))

    chunks = (0, 1)
    sent = {}
    moved = jnp.zeros((16, rows, width), BF16)
    grad_all = jnp.zeros((16, rows, hidden), BF16)

    def take(moved, grad_all, grad, step, chunk):
        spot = place(step, chunk)
        return put(moved, dot_rows(grad, in_weights).astype(BF16), spot), put(grad_all, grad, spot)

    for j in chunks:
        piece = grad[j * rows : (j + 1) * rows]
        moved, grad_all = take(moved, grad_all, piece, 0, j)
        sent[j] = [piece, piece]
    for step in (1, 2, 3):
        for j in chunks:
            from_0, from_1 = hop(sent[j][0], 0), hop(sent[j][1], 1)
            moved, grad_all = take(moved, grad_all, from_0, step, j)
            moved, grad_all = take(moved, grad_all, from_1, -step, j)
            sent[j] = [from_1, from_0]
    for j in chunks:
        ends = [hop(sent[j][s][s * half : (s + 1) * half], s) for s in (0, 1)]
        moved, grad_all = take(moved, grad_all, jnp.concatenate(ends, 0), 4, j)

    lines = moved.reshape(4, 4 * rows, width)
    goes = {k: at(lines, i2 ^ k) for k in range(4)}
    goes, ring[2], in_all = lax.optimization_barrier((goes, ring[2], in_all))
    mid = goes[0].astype(F32)
    for k in (2, 1, 3):
        mid = mid + lax.ppermute(goes[k], "row", plane_pairs(k, False)).astype(F32)
    grad_all = grad_all.reshape(16 * rows, hidden)
    turn()
    in_all, ring[3] = lax.optimization_barrier((in_all, ring[3]))
    in_other = dot_tokens(in_all, grad_all[:, units:])
    in_own = dot_tokens(in_all, grad_all[:, :units])
    mid, in_own, in_other = lax.optimization_barrier((mid.reshape(4, rows, width), in_own, in_other))
    from_0, from_1 = ring[3]
    ends = jnp.concatenate([hop(from_1[:rows], 0), hop(from_0[rows:], 1)], 0)
    active_all = put(jnp.zeros((8, 2 * rows, hidden), BF16), active, block_at(0))
    for step in (1, 2, 3):
        active_all = put(active_all, ring[step][0], block_at(step))
        active_all = put(active_all, ring[step][1], block_at(-step))
    active_all = put(active_all, ends, block_at(4))
    active_all = lax.cond(
        core == 0, lambda a: a, lambda a: jnp.swapaxes(a, 0, 1), active_all.reshape(4, 4, rows, hidden)
    ).reshape(16 * rows, hidden)
    out_other = dot_tokens(active_all[:, units:], cot_all)
    out_own = dot_tokens(active_all[:, :units], cot_all)
    entry_grad = in_own + swap(in_other)
    out_grad = out_own + swap(out_other)
    total = at(mid, i1)
    for k in (2, 1, 3):
        total = total + lax.ppermute(at(mid, i1 ^ k).astype(BF16), "row", plane_pairs(k, True)).astype(F32)
    total, entry_grad = lax.optimization_barrier((total, entry_grad))
    own, other = total[:half], swap(total[half:])
    token_grad = jnp.where(core == 0, jnp.concatenate([own, other], 0), jnp.concatenate([other, own], 0))
    return (token_grad, entry_grad, out_grad)


def solution(mesh):
    in_specs = (P("row", "col"), P("row", "col"), P("col", "row"), P("col", "row"), P("row", "col"))
    out_specs = (P("row", "col"), P("col", "row"), P("row", "col"))
    return jax.shard_map(body, mesh=mesh, in_specs=in_specs, out_specs=out_specs, check_vma=False)
```

```python
import jax
import jax.numpy as jnp
from jax import lax
from jax.sharding import PartitionSpec as P

root_half = 0.7071067811865476
inverse_root = 0.3989422804014327
F32 = jnp.float32
BF16 = jnp.bfloat16

CORE_SWAP = [(r, r ^ 1) for r in range(32)]
RING = ([(c, c ^ 1) for c in range(8)], [(c, (c - 1) % 8 if c % 2 == 0 else (c + 1) % 8) for c in range(8)])


def plane_pairs(k, first):
    pairs = []
    for r in range(32):
        y, x, core = r // 8, (r // 2) % 4, r % 2
        if (core == 0) == first:
            x ^= k
        else:
            y ^= k
        pairs.append((r, y * 8 + x * 2 + core))
    return pairs


def gelu_parts(saved):
    widened = saved.astype(F32)
    lower_mass = 0.5 * (1.0 + lax.erf(widened * root_half))
    density = inverse_root * jnp.exp(-0.5 * widened * widened)
    return (widened * lower_mass, lower_mass + widened * density)


def at(x, i):
    return lax.dynamic_index_in_dim(x, i, 0, keepdims=False)


def put(x, piece, i):
    return lax.dynamic_update_index_in_dim(x, piece, i, 0)


def after(x, *others):
    return lax.optimization_barrier((x,) + others)[0]


def swap(x):
    return lax.ppermute(x, "row", CORE_SWAP)


def hop(a, side):
    return lax.ppermute(a, "col", RING[side])


def dot_rows(a, b):
    return lax.dot_general(a, b, (((1,), (1,)), ((), ())), preferred_element_type=F32)


def dot_tokens(a, b):
    return lax.dot_general(a, b, (((0,), (0,)), ((), ())), preferred_element_type=F32)


def body(inputs, cotangent, saved_pre, weight_in, weight_out):
    row, col = lax.axis_index("row"), lax.axis_index("col")
    y, x, core = row // 8, (row // 2) % 4, row % 2
    i1 = jnp.where(core == 0, x, y)
    i2 = jnp.where(core == 0, y, x)
    sign = 1 - 2 * (col % 2)
    width, units = weight_in.shape
    rows = inputs.shape[0]
    half = rows // 2
    hidden = 2 * units

    def token_half(shard):
        return lax.dynamic_slice_in_dim(shard, core * half, half, 0)

    def pair_of(shard):
        return jnp.concatenate([token_half(shard), token_half(swap(shard))], 0)

    def gather_first(pair):
        line = {k: lax.ppermute(pair, "row", plane_pairs(k, True)) for k in (2, 1, 3)}
        line[0] = pair
        whole = jnp.zeros((4, rows, width), BF16)
        for k in (0, 2, 1, 3):
            whole = put(whole, line[k], i1 ^ k)
        return whole.reshape(4 * rows, width)

    def gather_second(line):
        lines = {k: lax.ppermute(line, "row", plane_pairs(k, False)) for k in (2, 1, 3)}
        lines[0] = line
        return lines

    def in_order(lines):
        whole = jnp.zeros((4, 4 * rows, width), BF16)
        for k in (0, 1, 3, 2):
            whole = put(whole, lines[k], i2 ^ k)
        return whole.reshape(16 * rows, width)

    cot_pair = pair_of(cotangent)
    cot_line = gather_first(cot_pair)
    weight_out_t, weight_in_t, inputs_t = lax.optimization_barrier((weight_out, weight_in, inputs, cot_pair))[:3]
    out_weights = jnp.concatenate([weight_out_t, swap(weight_out_t)], 0)

    def saved_half(block):
        split = block.reshape(2, 2, 2, half, units)
        split = lax.dynamic_index_in_dim(split, core, 2, keepdims=False)
        own = lax.dynamic_index_in_dim(split, core, 1, keepdims=False)
        other = lax.dynamic_index_in_dim(split, 1 - core, 1, keepdims=False)
        return jnp.concatenate([own, other], 1)

    saved_t = after(saved_pre, cot_pair)
    saved = jnp.concatenate([saved_half(saved_t), saved_half(swap(saved_t))], 2)
    active, slope = gelu_parts(saved)
    active, slope = lax.optimization_barrier((active.astype(BF16).reshape(2 * rows, hidden), slope))

    cot_lines = gather_second(cot_line)
    partial = jnp.zeros((4, 4 * rows, hidden), BF16)
    partial = put(partial, dot_rows(cot_lines[0], out_weights).astype(BF16), i2)
    active, partial = lax.optimization_barrier((active, partial))
    ring = [(active, active)]

    def turn():
        from_0, from_1 = ring[-1]
        ring.append((hop(from_1, 0), hop(from_0, 1)))

    turn()
    for k in (1, 3, 2):
        partial = put(partial, dot_rows(cot_lines[k], out_weights).astype(BF16), i2 ^ k)
    partial, ring[1] = lax.optimization_barrier((partial, ring[1]))
    partial = partial.reshape(16, rows, hidden)

    def block_at(step):
        return (col + step * sign) % 8

    def place(step, chunk):
        by, bx = block_at(step) // 2, 2 * (block_at(step) % 2) + chunk
        return jnp.where(core == 0, by * 4 + bx, bx * 4 + by)

    def part(step):
        return [at(partial, place(step, chunk)).astype(F32) for chunk in (0, 1)]

    def add(step, sum_0, sum_1):
        go_0, go_1 = part(step), part(-step)
        if step == 3:
            go_0[1], go_1[0] = go_0[1] + sum_1.astype(F32), go_1[0] + sum_0.astype(F32)
        else:
            go_0 = [g + sum_1[j * rows : (j + 1) * rows].astype(F32) for j, g in enumerate(go_0)]
            go_1 = [g + sum_0[j * rows : (j + 1) * rows].astype(F32) for j, g in enumerate(go_1)]
        return hop(jnp.concatenate(go_0, 0).astype(BF16), 0), hop(jnp.concatenate(go_1, 0).astype(BF16), 1)

    in_pair = pair_of(after(inputs_t, cot_lines[3]))
    sums = (hop(at(partial, place(4, 0)), 0), hop(at(partial, place(4, 1)), 1))
    turn()
    sums, ring[2], in_pair = lax.optimization_barrier((sums, ring[2], in_pair))

    sums = add(3, *sums)
    in_line = gather_first(in_pair)
    sums, in_line = lax.optimization_barrier((sums, in_line))

    in_lines = gather_second(in_line)
    sums = lax.optimization_barrier(add(2, *sums))

    sums = add(1, *sums)
    sums, in_lines = lax.optimization_barrier((sums, in_lines))
    summed = jnp.concatenate(part(0), 0) + sums[0].astype(F32) + sums[1].astype(F32)
    grad = (summed * slope.reshape(2 * rows, hidden)).astype(BF16)

    in_all = in_order(in_lines)
    cot_all = in_order(cot_lines)
    in_weights = jnp.concatenate([weight_in_t, swap(weight_in_t)], 1)

    grad, in_all, cot_all, in_weights = lax.optimization_barrier((grad, in_all, cot_all, in_weights))

    chunks = (0, 1)
    sent = {}
    moved = jnp.zeros((16, rows, width), BF16)
    grad_all = jnp.zeros((16, rows, hidden), BF16)

    def take(moved, grad_all, grad, step, chunk):
        spot = place(step, chunk)
        return put(moved, dot_rows(grad, in_weights).astype(BF16), spot), put(grad_all, grad, spot)

    for j in chunks:
        piece = grad[j * rows : (j + 1) * rows]
        moved, grad_all = take(moved, grad_all, piece, 0, j)
        sent[j] = [piece, piece]
    for step in (1, 2, 3):
        for j in chunks:
            from_0, from_1 = hop(sent[j][0], 0), hop(sent[j][1], 1)
            moved, grad_all = take(moved, grad_all, from_0, step, j)
            moved, grad_all = take(moved, grad_all, from_1, -step, j)
            sent[j] = [from_1, from_0]
    for j in chunks:
        ends = [hop(sent[j][s][s * half : (s + 1) * half], s) for s in (0, 1)]
        moved, grad_all = take(moved, grad_all, jnp.concatenate(ends, 0), 4, j)

    lines = moved.reshape(4, 4 * rows, width)
    goes = {k: at(lines, i2 ^ k) for k in range(4)}
    goes, ring[2], in_all = lax.optimization_barrier((goes, ring[2], in_all))
    mid = goes[0].astype(F32)
    for k in (2, 1, 3):
        mid = mid + lax.ppermute(goes[k], "row", plane_pairs(k, False)).astype(F32)
    grad_all = grad_all.reshape(16 * rows, hidden)
    turn()
    in_all, ring[3] = lax.optimization_barrier((in_all, ring[3]))
    in_other = dot_tokens(in_all, grad_all[:, units:])
    in_own = dot_tokens(in_all, grad_all[:, :units])
    mid, in_own, in_other = lax.optimization_barrier((mid.reshape(4, rows, width), in_own, in_other))
    from_0, from_1 = ring[3]
    ends = jnp.concatenate([hop(from_1[:rows], 0), hop(from_0[rows:], 1)], 0)
    active_all = put(jnp.zeros((8, 2 * rows, hidden), BF16), active, block_at(0))
    for step in (1, 2, 3):
        active_all = put(active_all, ring[step][0], block_at(step))
        active_all = put(active_all, ring[step][1], block_at(-step))
    active_all = put(active_all, ends, block_at(4))
    active_all = lax.cond(
        core == 0, lambda a: a, lambda a: jnp.swapaxes(a, 0, 1), active_all.reshape(4, 4, rows, hidden)
    ).reshape(16 * rows, hidden)
    out_other = dot_tokens(active_all[:, units:], cot_all)
    out_own = dot_tokens(active_all[:, :units], cot_all)
    entry_grad = in_own + swap(in_other)
    total = at(mid, i1)
    arrived = [lax.ppermute(at(mid, i1 ^ k).astype(BF16), "row", plane_pairs(k, True)) for k in (2, 1, 3)]
    arrived, entry_grad, out_own = lax.optimization_barrier((arrived, entry_grad, out_own))
    for piece in arrived:
        total = total + piece.astype(F32)
    out_grad = out_own + swap(out_other)
    own, other = total[:half], swap(total[half:])
    token_grad = jnp.where(core == 0, jnp.concatenate([own, other], 0), jnp.concatenate([other, own], 0))
    return (token_grad, entry_grad, out_grad)


def solution(mesh):
    in_specs = (P("row", "col"), P("row", "col"), P("col", "row"), P("col", "row"), P("row", "col"))
    out_specs = (P("row", "col"), P("col", "row"), P("row", "col"))
    return jax.shard_map(body, mesh=mesh, in_specs=in_specs, out_specs=out_specs, check_vma=False)
```

```python
import jax
import jax.numpy as jnp
from jax import lax
from jax.sharding import PartitionSpec as P

root_half = 0.7071067811865476
inverse_root = 0.3989422804014327
F32 = jnp.float32
BF16 = jnp.bfloat16

CORE_SWAP = [(r, r ^ 1) for r in range(32)]
RING = ([(c, c ^ 1) for c in range(8)], [(c, (c - 1) % 8 if c % 2 == 0 else (c + 1) % 8) for c in range(8)])


def plane_pairs(k, first):
    pairs = []
    for r in range(32):
        y, x, core = r // 8, (r // 2) % 4, r % 2
        if (core == 0) == first:
            x ^= k
        else:
            y ^= k
        pairs.append((r, y * 8 + x * 2 + core))
    return pairs


def gelu_parts(saved):
    widened = saved.astype(F32)
    lower_mass = 0.5 * (1.0 + lax.erf(widened * root_half))
    density = inverse_root * jnp.exp(-0.5 * widened * widened)
    return (widened * lower_mass, lower_mass + widened * density)


def at(x, i):
    return lax.dynamic_index_in_dim(x, i, 0, keepdims=False)


def put(x, piece, i):
    return lax.dynamic_update_index_in_dim(x, piece, i, 0)


def after(x, *others):
    return lax.optimization_barrier((x,) + others)[0]


def swap(x):
    return lax.ppermute(x, "row", CORE_SWAP)


def hop(a, side):
    return lax.ppermute(a, "col", RING[side])


def dot_rows(a, b):
    return lax.dot_general(a, b, (((1,), (1,)), ((), ())), preferred_element_type=F32)


def dot_tokens(a, b):
    return lax.dot_general(a, b, (((0,), (0,)), ((), ())), preferred_element_type=F32)


def body(inputs, cotangent, saved_pre, weight_in, weight_out):
    row, col = lax.axis_index("row"), lax.axis_index("col")
    y, x, core = row // 8, (row // 2) % 4, row % 2
    i1 = jnp.where(core == 0, x, y)
    i2 = jnp.where(core == 0, y, x)
    sign = 1 - 2 * (col % 2)
    width, units = weight_in.shape
    rows = inputs.shape[0]
    half = rows // 2
    hidden = 2 * units

    def token_half(shard):
        return lax.dynamic_slice_in_dim(shard, core * half, half, 0)

    def pair_of(shard):
        return jnp.concatenate([token_half(shard), token_half(swap(shard))], 0)

    def gather_first(pair):
        line = {k: lax.ppermute(pair, "row", plane_pairs(k, True)) for k in (2, 1, 3)}
        line[0] = pair
        whole = jnp.zeros((4, rows, width), BF16)
        for k in (0, 2, 1, 3):
            whole = put(whole, line[k], i1 ^ k)
        return whole.reshape(4 * rows, width)

    def gather_second(line):
        lines = {k: lax.ppermute(line, "row", plane_pairs(k, False)) for k in (2, 1, 3)}
        lines[0] = line
        return lines

    def in_order(lines):
        whole = jnp.zeros((4, 4 * rows, width), BF16)
        for k in (0, 1, 3, 2):
            whole = put(whole, lines[k], i2 ^ k)
        return whole.reshape(16 * rows, width)

    cot_pair = pair_of(cotangent)
    cot_line = gather_first(cot_pair)
    weight_out_t, weight_in_t, inputs_t = lax.optimization_barrier((weight_out, weight_in, inputs, cot_pair))[:3]
    out_weights = jnp.concatenate([weight_out_t, swap(weight_out_t)], 0)

    def saved_half(block):
        split = block.reshape(2, 2, 2, half, units)
        split = lax.dynamic_index_in_dim(split, core, 2, keepdims=False)
        own = lax.dynamic_index_in_dim(split, core, 1, keepdims=False)
        other = lax.dynamic_index_in_dim(split, 1 - core, 1, keepdims=False)
        return jnp.concatenate([own, other], 1)

    saved_t = after(saved_pre, cot_pair)
    saved = jnp.concatenate([saved_half(saved_t), saved_half(swap(saved_t))], 2)
    active, slope = gelu_parts(saved)
    active, slope = lax.optimization_barrier((active.astype(BF16).reshape(2 * rows, hidden), slope))

    cot_lines = gather_second(cot_line)
    partial = jnp.zeros((4, 4 * rows, hidden), BF16)
    partial = put(partial, dot_rows(cot_lines[0], out_weights).astype(BF16), i2)
    active, partial = lax.optimization_barrier((active, partial))
    ring = [(active, active)]

    def turn():
        from_0, from_1 = ring[-1]
        ring.append((hop(from_1, 0), hop(from_0, 1)))

    turn()
    for k in (1, 3, 2):
        partial = put(partial, dot_rows(cot_lines[k], out_weights).astype(BF16), i2 ^ k)
    partial, ring[1] = lax.optimization_barrier((partial, ring[1]))
    partial = partial.reshape(16, rows, hidden)

    def block_at(step):
        return (col + step * sign) % 8

    def place(step, chunk):
        by, bx = block_at(step) // 2, 2 * (block_at(step) % 2) + chunk
        return jnp.where(core == 0, by * 4 + bx, bx * 4 + by)

    def part(step):
        return [at(partial, place(step, chunk)).astype(F32) for chunk in (0, 1)]

    def add(step, sum_0, sum_1):
        go_0, go_1 = part(step), part(-step)
        if step == 3:
            go_0[1], go_1[0] = go_0[1] + sum_1.astype(F32), go_1[0] + sum_0.astype(F32)
        else:
            go_0 = [g + sum_1[j * rows : (j + 1) * rows].astype(F32) for j, g in enumerate(go_0)]
            go_1 = [g + sum_0[j * rows : (j + 1) * rows].astype(F32) for j, g in enumerate(go_1)]
        return hop(jnp.concatenate(go_0, 0).astype(BF16), 0), hop(jnp.concatenate(go_1, 0).astype(BF16), 1)

    in_pair = pair_of(after(inputs_t, cot_lines[3]))
    sums = (hop(at(partial, place(4, 0)), 0), hop(at(partial, place(4, 1)), 1))
    turn()
    sums, ring[2], in_pair = lax.optimization_barrier((sums, ring[2], in_pair))

    sums = add(3, *sums)
    in_line = gather_first(in_pair)
    sums, in_line = lax.optimization_barrier((sums, in_line))

    in_lines = gather_second(in_line)
    sums = lax.optimization_barrier(add(2, *sums))

    sums = add(1, *sums)
    sums, in_lines = lax.optimization_barrier((sums, in_lines))
    summed = jnp.concatenate(part(0), 0) + sums[0].astype(F32) + sums[1].astype(F32)
    grad = (summed * slope.reshape(2 * rows, hidden)).astype(BF16)

    in_all = in_order(in_lines)
    cot_all = in_order(cot_lines)
    in_weights = jnp.concatenate([weight_in_t, swap(weight_in_t)], 1)

    grad, in_all, cot_all, in_weights = lax.optimization_barrier((grad, in_all, cot_all, in_weights))

    chunks = (0, 1)
    sent = {}
    moved = jnp.zeros((16, rows, width), BF16)
    grad_all = jnp.zeros((16, rows, hidden), BF16)

    def take(moved, grad_all, grad, step, chunk):
        spot = place(step, chunk)
        return put(moved, dot_rows(grad, in_weights).astype(BF16), spot), put(grad_all, grad, spot)

    for j in chunks:
        piece = grad[j * rows : (j + 1) * rows]
        moved, grad_all = take(moved, grad_all, piece, 0, j)
        sent[j] = [piece, piece]
    for step in (1, 2, 3):
        for j in chunks:
            from_0, from_1 = hop(sent[j][0], 0), hop(sent[j][1], 1)
            moved, grad_all = take(moved, grad_all, from_0, step, j)
            moved, grad_all = take(moved, grad_all, from_1, -step, j)
            sent[j] = [from_1, from_0]
    for j in chunks:
        ends = [hop(sent[j][s][s * half : (s + 1) * half], s) for s in (0, 1)]
        moved, grad_all = take(moved, grad_all, jnp.concatenate(ends, 0), 4, j)

    lines = moved.reshape(4, 4 * rows, width)
    goes = {k: at(lines, i2 ^ k) for k in range(4)}
    goes, ring[2], in_all = lax.optimization_barrier((goes, ring[2], in_all))
    mid = goes[0].astype(F32)
    for k in (2, 1, 3):
        mid = mid + lax.ppermute(goes[k], "row", plane_pairs(k, False)).astype(F32)
    grad_all = grad_all.reshape(16 * rows, hidden)
    turn()
    in_all = after(in_all, swap(goes[3][:16]))
    in_other = dot_tokens(in_all, grad_all[:, units:])
    in_own = dot_tokens(in_all, grad_all[:, :units])
    mid, in_own, in_other = lax.optimization_barrier((mid.reshape(4, rows, width), in_own, in_other))
    from_0, from_1 = ring[3]
    ends = jnp.concatenate([hop(from_1[:rows], 0), hop(from_0[rows:], 1)], 0)
    active_all = put(jnp.zeros((8, 2 * rows, hidden), BF16), active, block_at(0))
    for step in (1, 2, 3):
        active_all = put(active_all, ring[step][0], block_at(step))
        active_all = put(active_all, ring[step][1], block_at(-step))
    active_all = put(active_all, ends, block_at(4))
    active_all = lax.cond(
        core == 0, lambda a: a, lambda a: jnp.swapaxes(a, 0, 1), active_all.reshape(4, 4, rows, hidden)
    ).reshape(16 * rows, hidden)
    out_other = dot_tokens(active_all[:, units:], cot_all)
    out_own = dot_tokens(active_all[:, :units], cot_all)
    entry_grad = in_own + swap(in_other)
    total = at(mid, i1)
    arrived = [lax.ppermute(at(mid, i1 ^ k).astype(BF16), "row", plane_pairs(k, True)) for k in (2, 1, 3)]
    arrived, entry_grad, out_own = lax.optimization_barrier((arrived, entry_grad, out_own))
    for piece in arrived:
        total = total + piece.astype(F32)
    out_grad = out_own + swap(out_other)
    own, other = total[:half], swap(total[half:])
    token_grad = jnp.where(core == 0, jnp.concatenate([own, other], 0), jnp.concatenate([other, own], 0))
    return (token_grad, entry_grad, out_grad)


def solution(mesh):
    in_specs = (P("row", "col"), P("row", "col"), P("col", "row"), P("col", "row"), P("row", "col"))
    out_specs = (P("row", "col"), P("col", "row"), P("row", "col"))
    return jax.shard_map(body, mesh=mesh, in_specs=in_specs, out_specs=out_specs, check_vma=False)
```
